256 devices in a mesh: comp: 16 (over y, z_hi), freq: 16 (over z_lo, x, core).
Axes of the slice: x: 4, y: 4, z: 8 (z_hi: 4, z_lo: 2; z = z_hi * 2 + z_lo), core: 2. Of those that a mesh axis runs over, the one named last changes fastest.
Arguments:
- station_uvw: float32 [3, 512], replicated, may hold values from -1792 to 1792
- directions: float32 [2, 4096], P(None, 'comp'), may hold values from -0.1 to 0.1
- flux_ref: float32 [4096], P('comp'), may hold values from 0.2 to 2
- spectral_index: float32 [4096], P('comp'), may hold values from -1.5 to 0.5
- channel_index: int32 [32], P('freq'), may hold values from 0 to 4095
- slot_pair: int32 [528], replicated, may hold values from 0 to 527, each once
- observed: float32 [32, 528, 512], P('freq', 'comp'), may hold values from -6 to 6
Outputs:
- residual: float32 [32, 528, 512], P('freq', 'comp')
- flux_grad: float32 [4096], P('comp')
The draws below stay inside these ranges and needn't reach their ends.
Inputs may be any that keep to these rules, and one draw needn't show every extreme that they name: slot_pair[k] is the pair index held at slot k; every pair is held once; slots k * 33 to (k + 1) * 33 - 1 lie on index k of comp.
All inputs are finite; a program needn't handle non-finite values.
Results may differ from the reference program's by a relative error of at most 0.0059.
Values sent between devices are 32-bit elements; how exact they have to be, the bound alone decides.
No kernel may reach another device: no remote copies, remote signals or barrier semaphores. Data moves between devices by JAX's collectives and lax.ppermute only.
A program may use at most 128 MiB of HBM per device.

```python
import math
import jax
import jax.numpy as jnp
import numpy as np
from jax import lax

NS = 512
NB = 32
BS = 16
NPAIR = 528
COMPS = 4096
CHANNELS = 32


def touch_ends(array, key, low, top_value):
    longest = array.shape.index(max(array.shape))
    spots = []
    for shift in (0, 1):
        where = [jax.random.randint(jax.random.fold_in(key, axis), (), 0, length) for axis, length in enumerate(array.shape)]
        where[longest] = (where[longest] + shift) % array.shape[longest]
        spots.append(tuple(where))
    return array.at[spots[0]].set(low).at[spots[1]].set(top_value)


def levels(rng, dims, split, low, largest):
    gain = 1.0
    for dim, blocks in split:
        heights = jax.random.uniform(jax.random.fold_in(jax.random.fold_in(rng, 6), dim), (blocks,), jnp.float32, low / len(split), largest / len(split))
        gain = gain * jnp.repeat(jnp.exp(heights), dims[dim] // blocks).reshape((-1,) + (1,) * (len(dims) - 1 - dim))
    return gain


def scatter_about(own_key, dims, scale, bound, cuts=(), kind=jnp.bfloat16):
    values = jax.random.normal(own_key, dims, jnp.float32) * scale
    if len(cuts) > 0:
        values = levels(own_key, dims, cuts, -0.22, 0.18) * values
    return jnp.clip(values, min=-bound, max=bound).astype(kind)


def setup_inputs(seed: int = 0) -> dict:
    key_of = jax.random.split(jax.random.key(seed), 8)
    station_uvw = scatter_about(key_of[0], (3, NS), 300.0, 1792.0, (), jnp.float32)
    directions = jnp.clip(jax.random.uniform(key_of[1], (2, COMPS), jnp.float32, -0.1, 0.1) * levels(key_of[1], (2, COMPS), ((1, 16),), -0.4, 0.0), -0.1, 0.1)
    flux_ref = jnp.clip(jnp.exp(math.log(2.0) - 2.3025851 * jax.random.uniform(key_of[2], (COMPS,), jnp.float32) ** levels(key_of[2], (COMPS,), ((0, 16),), -0.2, 0.2)), 0.2, 2.0)
    spectral_index = jnp.clip(-1.5 + 2.0 * jax.random.uniform(key_of[3], (COMPS,), jnp.float32) ** levels(key_of[3], (COMPS,), ((0, 16),), -0.2, 0.2), -1.5, 0.5)
    channel_index = touch_ends(jax.random.randint(key_of[4], (CHANNELS,), 0, 4096), jax.random.fold_in(key_of[4], 1), 0, 4095).astype(jnp.int32)
    slot_pair = jax.random.permutation(key_of[5], NPAIR).astype(jnp.int32)
    observed = scatter_about(key_of[6], (CHANNELS, NPAIR, 2 * BS * BS), 1.0, 6.0, ((0, 16), (1, 16)), jnp.float32)
    return dict(station_uvw=station_uvw, directions=directions, flux_ref=flux_ref, spectral_index=spectral_index, channel_index=channel_index, slot_pair=slot_pair, observed=observed)


def pair_tables(blocks):
    first, second = np.triu_indices(blocks)
    row_ids = np.arange(blocks)[:, None]
    col_ids = np.arange(blocks)[None, :]
    low_ids = np.minimum(row_ids, col_ids)
    high_ids = np.maximum(row_ids, col_ids)
    grid = low_ids * blocks - low_ids * (low_ids - 1) // 2 + high_ids - low_ids
    return (first.astype(np.int32), second.astype(np.int32), grid.astype(np.int32))

def phasor_pair(station_uvw, directions, freq_ratio):
    l_part = directions[0]
    m_part = directions[1]
    w_term = jnp.sqrt(1.0 - l_part * l_part - m_part * m_part) - 1.0
    path_len = station_uvw[0][:, None] * l_part[None, :] + station_uvw[1][:, None] * m_part[None, :] + station_uvw[2][:, None] * w_term[None, :]
    angles = 2.0 * math.pi * freq_ratio * path_len
    return (jnp.cos(angles).astype(jnp.bfloat16), (-jnp.sin(angles)).astype(jnp.bfloat16))

def model_matrix(weighted_re, weighted_im, phase_re, phase_im):
    stations = phase_re.shape[0]
    left = jnp.concatenate([jnp.concatenate([weighted_re, weighted_im], axis=1), jnp.concatenate([weighted_im, -weighted_re], axis=1)], axis=0)
    right = jnp.concatenate([phase_re, phase_im], axis=1)
    stacked_model = lax.dot_general(left, right, (((1,), (1,)), ((), ())), preferred_element_type=jnp.float32)
    return (stacked_model[:stations], stacked_model[stations:])

def pick_blocks(matrix, row_block, col_block, blocks, side_len):
    block_grid = matrix.reshape(blocks, side_len, blocks, side_len).transpose(0, 2, 1, 3)
    block_grid = block_grid.reshape(blocks * blocks, side_len, side_len)
    return block_grid[row_block * blocks + col_block]

def residual_blocks(model_re, model_im, observed, on_diag, side_len):
    shaped = observed.reshape(observed.shape[:-1] + (2, side_len, side_len))
    above = jnp.arange(side_len)[:, None] < jnp.arange(side_len)[None, :]
    part_re = jnp.where(above, shaped[..., 0, :, :], 0.0)
    part_im = jnp.where(above, shaped[..., 1, :, :], 0.0)
    herm_re = part_re + jnp.swapaxes(part_re, -1, -2)
    herm_im = part_im - jnp.swapaxes(part_im, -1, -2)
    flag = on_diag[:, None, None]
    ref_re = jnp.where(flag, herm_re, shaped[..., 0, :, :])
    ref_im = jnp.where(flag, herm_im, shaped[..., 1, :, :])
    autos = flag & (jnp.arange(side_len)[:, None] == jnp.arange(side_len)[None, :])
    res_re = jnp.where(autos, 0.0, model_re - ref_re)
    res_im = jnp.where(autos, 0.0, model_im - ref_im)
    flat_shape = res_re.shape[:-2] + (side_len * side_len,)
    return jnp.concatenate([res_re.reshape(flat_shape), res_im.reshape(flat_shape)], axis=-1)

def hermitian_matrix(slot_rows, slot_pair, blocks, side_len):
    first, second, grid = pair_tables(blocks)
    chans = slot_rows.shape[0]
    canonical = jnp.zeros_like(slot_rows).at[:, slot_pair].set(slot_rows)
    arranged = canonical[:, jnp.asarray(grid.reshape(-1))]
    arranged = arranged.reshape(chans, blocks, blocks, 2, side_len, side_len)
    below = jnp.asarray(np.arange(blocks)[:, None] > np.arange(blocks)[None, :])[None, :, :, None, None]
    part_re = jnp.where(below, jnp.swapaxes(arranged[:, :, :, 0], -1, -2), arranged[:, :, :, 0])
    part_im = jnp.where(below, -jnp.swapaxes(arranged[:, :, :, 1], -1, -2), arranged[:, :, :, 1])
    total = blocks * side_len
    matrix_re = part_re.transpose(0, 1, 3, 2, 4).reshape(chans, total, total)
    matrix_im = part_im.transpose(0, 1, 3, 2, 4).reshape(chans, total, total)
    return (matrix_re, matrix_im)

def contract(matrix_re, matrix_im, phase_re, phase_im):
    top_half = jnp.concatenate([matrix_re, -matrix_im], axis=1)
    bottom_half = jnp.concatenate([matrix_im, matrix_re], axis=1)
    stacked = jnp.concatenate([phase_re, phase_im], axis=0)
    product = jnp.dot(jnp.concatenate([top_half, bottom_half], axis=0), stacked, preferred_element_type=jnp.float32)
    return lax.optimization_barrier(jnp.sum(stacked.astype(jnp.float32) * product, axis=0))

def reference(station_uvw, directions, flux_ref, spectral_index, channel_index, slot_pair, observed):
    first, second, grid = pair_tables(NB)
    row_block = jnp.asarray(first)[slot_pair]
    col_block = jnp.asarray(second)[slot_pair]
    on_diag = row_block == col_block
    side_len = NS // NB
    scale = 1.0 / math.sqrt(COMPS)

    def one_channel(inputs):
        index_value, observed_rows = inputs
        freq_ratio = 1.0 + index_value.astype(jnp.float32) / 4096.0
        phase_re, phase_im = phasor_pair(station_uvw, directions, freq_ratio)
        spectral = freq_ratio ** spectral_index
        spectrum = flux_ref * spectral * scale
        weighted_re = (spectrum * phase_re.astype(jnp.float32)).astype(jnp.bfloat16)
        weighted_im = (spectrum * phase_im.astype(jnp.float32)).astype(jnp.bfloat16)
        model_re, model_im = model_matrix(weighted_re, weighted_im, phase_re, phase_im)
        residual_rows = residual_blocks(pick_blocks(model_re, row_block, col_block, NB, side_len), pick_blocks(model_im, row_block, col_block, NB, side_len), observed_rows, on_diag, side_len)
        matrix_re, matrix_im = hermitian_matrix(residual_rows[None], slot_pair, NB, side_len)
        terms = contract(matrix_re[0].astype(jnp.bfloat16), matrix_im[0].astype(jnp.bfloat16), phase_re, phase_im)
        return (residual_rows, terms * spectral)
    residual, terms = lax.map(one_channel, (channel_index, observed))
    flux_grad = lax.optimization_barrier(jnp.sum(terms, axis=0)) / (NS * CHANNELS)
    return (residual, flux_grad)
```

```python
import math

import jax
import jax.numpy as jnp
import numpy as np
from jax import lax
from jax.experimental import pallas as pl
from jax.experimental.pallas import tpu as pltpu
from jax.sharding import PartitionSpec as P

NB = 32
GROUP = 8
CHUNK = 256
MAGIC = 12582912.0
SIN_COEF = tuple(
    k * (1.0 - 2.0e-6) for k in (3.14158202, -5.16714276, 2.54189867, -0.55463514)
)


def split3(x):
    hi = lax.reduce_precision(x, 8, 7)
    rest = x - hi
    mid = lax.reduce_precision(rest, 8, 7)
    low = lax.reduce_precision(rest - mid, 8, 7)
    return hi, mid, low


def kernel(ib_ref, jb_ref, lhs_ref, d_ref, ref_ref, res_ref, grad_ref, q_ref, p_ref, g_ref):
    chans = lhs_ref.shape[0]
    comps = d_ref.shape[1]
    slots = ib_ref.shape[0]
    side = 16
    two = 2 * side
    groups = [(g, min(GROUP, slots - g)) for g in range(0, slots, GROUP)]
    width = GROUP * two

    def stack(ref, first, count, cols):
        return jnp.concatenate(
            [q_ref[ref[first + k], :, cols] for k in range(count)], axis=0
        )

    for ch in range(chans):

        @pl.loop(0, comps // CHUNK)
        def _(c):
            cols = pl.ds(pl.multiple_of(c * CHUNK, CHUNK), CHUNK)
            d = d_ref[:, cols]
            hi = d.astype(jnp.bfloat16).astype(jnp.float32)
            rest = d - hi
            mid = rest.astype(jnp.bfloat16).astype(jnp.float32)
            low = (rest - mid).astype(jnp.bfloat16).astype(jnp.float32)
            rhs = jnp.concatenate([hi, mid, low, hi, mid, hi], axis=0).astype(jnp.bfloat16)
            gain = d[3 + ch : 4 + ch]
            root = jnp.sqrt(2.0 * gain)
            coef = [jnp.broadcast_to(-k * root, (8, CHUNK))[None] for k in SIN_COEF]
            gain1 = jnp.broadcast_to(gain, (8, CHUNK))[None]
            gain2 = 2.0 * gain1
            rows = 64
            for r in range(0, lhs_ref.shape[1], rows):
                t = jnp.dot(
                    lhs_ref[ch, r : r + rows], rhs, preferred_element_type=jnp.float32
                ).reshape(rows // 8, 8, CHUNK)
                x = t - ((t + MAGIC) - MAGIC)
                z = x * x
                s = x * (coef[0] + z * (coef[1] + z * (coef[2] + z * coef[3])))
                y = s * s
                w = gain2 - y
                co = w * lax.rsqrt(w)
                im = (s * co).astype(jnp.bfloat16).reshape(rows // side, side, CHUNK)
                re = (gain1 - y).astype(jnp.bfloat16).reshape(rows // side, side, CHUNK)
                b = r // side
                q_ref[b : b + rows // side, 0:side, cols] = re
                q_ref[b : b + rows // side, side:two, cols] = im

        for gi, (first, count) in enumerate(groups):
            size = count * two
            kc = 512
            p_ref[0:size, 0:size] = jnp.zeros((size, size), jnp.float32)

            @pl.loop(0, comps // kc)
            def _(c):
                cols = pl.ds(pl.multiple_of(c * kc, kc), kc)
                a = stack(ib_ref, first, count, cols)
                b = stack(jb_ref, first, count, cols)
                p_ref[0:size, 0:size] += lax.dot_general(
                    a, b, (((1,), (1,)), ((), ())), preferred_element_type=jnp.float32
                )

            lane = lax.broadcasted_iota(jnp.int32, (two, 128), 1)
            row = lax.broadcasted_iota(jnp.int32, (two, 128), 0)
            top = row < side
            for k in range(count):
                base = k * two
                blk = p_ref[base : base + two, (base // 128) * 128 : (base // 128) * 128 + 128]
                if base % 128:
                    blk = pltpu.roll(blk, 128 - base % 128, 1)
                swap = jnp.concatenate([blk[side:], blk[:side]], axis=0)
                swap = pltpu.roll(swap, 128 - side, 1)
                model = blk + jnp.where(top, swap, -swap)
                diag = ib_ref[first + k] == jb_ref[first + k]
                mod_row = jnp.where(top, row, row - side)
                res = model[:, :side] - ref_ref[ch, first + k]
                zero = (mod_row[:, :side] == lane[:, :side]) & diag
                res = jnp.where(zero, 0.0, res)
                res_ref[ch, first + k] = res
                scaled = res * jnp.where(diag, 1.0, 2.0)
                other = jnp.concatenate([-scaled[side:], scaled[:side]], axis=0)
                full = jnp.concatenate([scaled, other], axis=1)
                pieces = [jnp.zeros((two, two * k), jnp.float32)] if k else []
                pieces.append(full)
                if k < count - 1:
                    pieces.append(jnp.zeros((two, two * (count - 1 - k)), jnp.float32))
                line = jnp.concatenate(pieces, axis=1) if len(pieces) > 1 else full
                g_ref[gi, base : base + two, 0:size] = line.astype(jnp.bfloat16)

        @pl.loop(0, comps // CHUNK)
        def _(c):
            cols = pl.ds(pl.multiple_of(c * CHUNK, CHUNK), CHUNK)
            acc = jnp.zeros((8, CHUNK), jnp.float32)
            for gi, (first, count) in enumerate(groups):
                size = count * two
                a = stack(ib_ref, first, count, cols)
                b = stack(jb_ref, first, count, cols)
                m = jnp.dot(g_ref[gi, 0:size, 0:size], b, preferred_element_type=jnp.float32)
                prod = a.astype(jnp.float32) * m
                acc = acc + jnp.sum(prod.reshape(size // 8, 8, CHUNK), axis=0)
            if ch == 0:
                grad_ref[:, cols] = acc
            else:
                grad_ref[:, cols] += acc


def device_kernel(ib, jb, lhs, d, ref):
    chans, stations, _ = lhs.shape
    comps = d.shape[1]
    slots = ref.shape[1]
    vm = pl.BlockSpec(memory_space=pltpu.VMEM)
    sm = pl.BlockSpec(memory_space=pltpu.SMEM)
    width = GROUP * 32
    ngroup = -(-slots // GROUP)
    return pl.pallas_call(
        kernel,
        out_shape=(
            jax.ShapeDtypeStruct(ref.shape, jnp.float32),
            jax.ShapeDtypeStruct((8, comps), jnp.float32),
        ),
        in_specs=[sm, sm, vm, vm, vm],
        out_specs=(vm, vm),
        scratch_shapes=[
            pltpu.VMEM((NB, 32, comps), jnp.bfloat16),
            pltpu.VMEM((width, width), jnp.float32),
            pltpu.VMEM((ngroup, width, width), jnp.bfloat16),
        ],
        compiler_params=pltpu.CompilerParams(vmem_limit_bytes=40 * 2**20),
        name="visibility",
    )(ib, jb, lhs, d, ref)


def station_factors(station_uvw, ratios):
    scaled = ratios[:, None, None] * station_uvw.T[None]
    hi, mid, low = split3(jnp.pad(scaled, ((0, 0), (0, 0), (0, 5))))
    return jnp.concatenate([hi, hi, hi, mid, mid, low], axis=-1).astype(jnp.bfloat16)


def component_rows(directions, flux_ref, spectral_index, ratios, scale):
    l_part = directions[0]
    m_part = directions[1]
    w_term = jnp.sqrt(1.0 - l_part * l_part - m_part * m_part) - 1.0
    gains = [
        jnp.sqrt(flux_ref * ratios[k] ** spectral_index * scale) for k in range(ratios.shape[0])
    ]
    rows = [l_part, m_part, w_term] + gains
    rows += [jnp.zeros_like(l_part)] * (8 - len(rows))
    return jnp.stack(rows, axis=0)


def slot_tables(own_pairs):
    starts = np.asarray([i * NB - i * (i - 1) // 2 for i in range(NB)], np.int32)
    row = jnp.sum((own_pairs[:, None] >= jnp.asarray(starts)[None, :]).astype(jnp.int32), axis=1) - 1
    col = own_pairs - (row * NB - row * (row - 1) // 2) + row
    return row, col


def reference_blocks(observed, on_diag, side):
    chans, slots, _ = observed.shape
    shaped = observed.reshape(chans, slots, 2, side, side)
    above = jnp.asarray(np.arange(side)[:, None] < np.arange(side)[None, :])
    part = jnp.where(above, shaped, 0.0)
    turned = jnp.swapaxes(part, -1, -2)
    herm = jnp.stack([part[:, :, 0] + turned[:, :, 0], part[:, :, 1] - turned[:, :, 1]], axis=2)
    out = jnp.where(on_diag[None, :, None, None, None], herm, shaped)
    return out.reshape(chans, slots, 2 * side, side)


def swap_perm(count, k):
    return [(i, i ^ k) for i in range(count)]


def gather_components(own, count):
    me = lax.axis_index("comp")
    parts = {0: own}
    for k in (1, 2, 3):
        parts[k] = lax.ppermute(own, "comp", swap_perm(count, k))
    low = jnp.stack([parts[k] for k in range(4)], axis=0)
    rounds = {0: low}
    for k in (4, 8, 12):
        rounds[k] = lax.ppermute(low, "comp", swap_perm(count, k))
    return jnp.stack([rounds[k] for k in (0, 4, 8, 12)], axis=0)


def body(station_uvw, directions, flux_ref, spectral_index, channel_index, slot_pair, observed):
    comp_count = lax.axis_size("comp")
    group_count = lax.axis_size("freq")
    stations = station_uvw.shape[1]
    side = stations // NB
    chans = channel_index.shape[0]
    own_slots = observed.shape[1]
    per_block = directions.shape[1]
    total = per_block * comp_count
    scale = 1.0 / math.sqrt(total)
    me = lax.axis_index("comp")
    ratios = 1.0 + channel_index.astype(jnp.float32) / 4096.0

    own = component_rows(directions, flux_ref, spectral_index, ratios, scale)
    d = gather_components(own, comp_count)
    d = d.reshape(comp_count, 8, per_block).transpose(1, 0, 2).reshape(8, total)

    own_pairs = lax.dynamic_slice_in_dim(slot_pair, me * own_slots, own_slots)
    ib, jb = slot_tables(own_pairs)
    ref = reference_blocks(observed, ib == jb, side)
    lhs = station_factors(station_uvw, ratios)
    res, grad = device_kernel(ib, jb, lhs, d, ref)
    residual = res.reshape(chans, own_slots, 2 * side * side)

    part = jnp.sum(grad, axis=0).reshape(comp_count, per_block)
    order = me ^ jnp.arange(comp_count)
    part = part[order]
    sent = jnp.broadcast_to(part[:, None, :], (comp_count, group_count, per_block))
    sent = sent.reshape(comp_count * group_count, per_block)
    got = lax.all_to_all(sent, ("comp", "freq"), 0, 0, tiled=True)
    flux_grad = jnp.sum(got, axis=0) / (flux_ref * (scale * stations * chans * group_count))
    return residual, flux_grad


def solution(mesh):
    in_specs = (P(), P(None, "comp"), P("comp"), P("comp"), P("freq"), P(), P("freq", "comp", None))
    out_specs = (P("freq", "comp", None), P("comp"))
    return jax.shard_map(body, mesh=mesh, in_specs=in_specs, out_specs=out_specs, check_vma=False)
```

```python
import math

import jax
import jax.numpy as jnp
import numpy as np
from jax import lax
from jax.experimental import pallas as pl
from jax.experimental.pallas import tpu as pltpu
from jax.sharding import PartitionSpec as P

NB = 32
GROUP = 8
CHUNK = 512
ROWS = 64
SIN_COEF = tuple(
    k * (1.0 - 2.0e-6) for k in (3.14158202, -5.16714276, 2.54189867, -0.55463514)
)


def pieces(x):
    hi = x.astype(jnp.bfloat16).astype(jnp.float32)
    rest = x - hi
    mid = rest.astype(jnp.bfloat16).astype(jnp.float32)
    low = (rest - mid).astype(jnp.bfloat16).astype(jnp.float32)
    return hi, mid, low


def kernel(
    ib_ref, jb_ref, dest_ref, ratio_ref, uvw_ref, d_ref, ref_ref, res_ref, sent_ref, lhs_ref, acc_ref, *rest
):
    chans, slots, two, side = ref_ref.shape
    blocks, _, width = d_ref.shape
    stations = uvw_ref.shape[1]
    copies = sent_ref.shape[0] // blocks
    comps = blocks * width
    scale = 1.0 / math.sqrt(comps)
    steps = comps // CHUNK
    per = CHUNK // width
    groups = [(g, min(GROUP, slots - g)) for g in range(0, slots, GROUP)]
    count_g = len(groups)
    p_refs = rest[: chans * count_g]
    g_refs = rest[chans * count_g : 2 * chans * count_g]
    q_refs = rest[2 * chans * count_g :]

    def stack(q_ref, ref, first, count):
        return jnp.concatenate([q_ref[ref[first + k]] for k in range(count)], axis=0)

    def stations_of(ch):
        uvw = jnp.concatenate(
            [uvw_ref[...] * ratio_ref[0, ch], jnp.zeros((5, stations), jnp.float32)], axis=0
        )
        hi, mid, low = pieces(uvw)
        rows = jnp.concatenate([hi, hi, hi, mid, mid, low], axis=0)
        lhs_ref[ch] = rows.T.astype(jnp.bfloat16)

    def phasors(ch, step):
        q_ref = q_refs[ch * steps + step]
        d = jnp.concatenate([d_ref[step * per + k] for k in range(per)], axis=1)
        l_part, m_part = d[0:1], d[1:2]
        w_term = jnp.sqrt(1.0 - l_part * l_part - m_part * m_part) - 1.0
        row = lax.broadcasted_iota(jnp.int32, d.shape, 0)
        hi, mid, low = pieces(jnp.where(row == 2, w_term, d))
        rhs = jnp.concatenate([hi, mid, low, hi, mid, hi], axis=0).astype(jnp.bfloat16)
        gain = jnp.sqrt(d[3:4] * jnp.exp2(d[4:5] * ratio_ref[1, ch]) * scale)
        root = jnp.sqrt(2.0 * gain)
        coef = [jnp.broadcast_to(-k * root, (8, CHUNK))[None] for k in SIN_COEF]
        gain1 = jnp.broadcast_to(gain, (8, CHUNK))[None]
        gain2 = 2.0 * gain1
        for r in range(0, stations, ROWS):
            t = jnp.dot(
                lhs_ref[ch, r : r + ROWS], rhs, preferred_element_type=jnp.float32
            ).reshape(ROWS // 8, 8, CHUNK)
            x = t - jnp.round(t)
            z = x * x
            poly = coef[-1]
            for k in coef[-2::-1]:
                poly = k + z * poly
            s = x * poly
            y = s * s
            w = gain2 - y
            co = w * lax.rsqrt(w)
            im = (s * co).astype(jnp.bfloat16).reshape(ROWS // side, side, CHUNK)
            re = (gain1 - y).astype(jnp.bfloat16).reshape(ROWS // side, side, CHUNK)
            b = r // side
            q_ref[b : b + ROWS // side, 0:side] = re
            q_ref[b : b + ROWS // side, side:two] = im

    def model(ch, step):
        q_ref = q_refs[ch * steps + step]
        for gi, (first, count) in enumerate(groups):
            size = count * two
            part = lax.dot_general(
                stack(q_ref, ib_ref, first, count),
                stack(q_ref, jb_ref, first, count),
                (((1,), (1,)), ((), ())),
                preferred_element_type=jnp.float32,
            )
            p_ref = p_refs[ch * count_g + gi]
            if step == 0:
                p_ref[0:size, 0:size] = part
            else:
                p_ref[0:size, 0:size] += part

    def residuals(ch):
        lane = lax.broadcasted_iota(jnp.int32, (two, 128), 1)
        row = lax.broadcasted_iota(jnp.int32, (two, 128), 0)
        top = row < side
        auto = jnp.where(top, row, row - side) == lane
        pad = jnp.zeros((two, 128 - side), jnp.float32)
        for gi, (first, count) in enumerate(groups):
            p_ref = p_refs[ch * count_g + gi]
            g_ref = g_refs[ch * count_g + gi]
            g_ref[...] = jnp.zeros(g_ref.shape, g_ref.dtype)
            for k in range(count):
                base = k * two
                window = (base // 128) * 128
                shift = base % 128
                blk = p_ref[base : base + two, window : window + 128]
                if shift:
                    blk = pltpu.roll(blk, 128 - shift, 1)
                swap = jnp.concatenate([blk[side:], -blk[:side]], axis=0)
                swap = pltpu.roll(swap, 128 - side, 1)
                diag = ib_ref[first + k] == jb_ref[first + k]
                seen = jnp.concatenate([ref_ref[ch, first + k], pad], axis=1)
                res = blk + swap - seen
                res = jnp.where((lane >= side) | (auto & diag), 0.0, res)
                res_ref[ch, first + k] = res[:, :side]
                scaled = res * jnp.where(diag, 1.0, 2.0)
                other = jnp.concatenate([-scaled[side:], scaled[:side]], axis=0)
                full = scaled + pltpu.roll(other, side, 1)
                if shift:
                    full = pltpu.roll(full, shift, 1)
                g_ref[base : base + two, window : window + 128] = full.astype(jnp.bfloat16)

    def gradient(ch, step):
        q_ref = q_refs[ch * steps + step]
        acc = jnp.zeros((8, CHUNK), jnp.float32)
        for gi, (first, count) in enumerate(groups):
            size = count * two
            m = jnp.dot(
                g_refs[ch * count_g + gi][0:size, 0:size],
                stack(q_ref, jb_ref, first, count),
                preferred_element_type=jnp.float32,
            )
            m = stack(q_ref, ib_ref, first, count).astype(jnp.float32) * m
            acc = acc + jnp.sum(m.reshape(size // 8, 8, CHUNK), axis=0)
        if ch > 0:
            acc = acc + acc_ref[step]
        if ch < chans - 1:
            acc_ref[step] = acc
            return
        total = jnp.sum(acc, axis=0, keepdims=True)
        for k in range(per):
            line = total[:, k * width : (k + 1) * width]
            sent_ref[pl.ds(dest_ref[step * per + k] * copies, copies)] = jnp.broadcast_to(
                line[None], (copies, 1, width)
            )

    for ch in range(chans):
        stations_of(ch)
    for ch in range(chans):
        for step in range(steps):
            phasors(ch, step)
            if step > 0:
                model(ch, step - 1)
                if ch > 0:
                    gradient(ch - 1, step - 1)
            elif ch > 0:
                model(ch - 1, steps - 1)
                residuals(ch - 1)
    last = chans - 1
    model(last, steps - 1)
    if last > 0:
        gradient(last - 1, steps - 1)
    residuals(last)
    for step in range(steps):
        gradient(last, step)


def device_kernel(ib, jb, dest, ratio, uvw, d, ref, copies):
    chans, slots, two, _ = ref.shape
    blocks, _, width = d.shape
    stations = uvw.shape[1]
    steps = blocks * width // CHUNK
    vm = pl.BlockSpec(memory_space=pltpu.VMEM)
    sm = pl.BlockSpec(memory_space=pltpu.SMEM)
    side = GROUP * two
    count = chans * -(-slots // GROUP)
    return pl.pallas_call(
        kernel,
        out_shape=(
            jax.ShapeDtypeStruct(ref.shape, jnp.float32),
            jax.ShapeDtypeStruct((blocks * copies, 1, width), jnp.float32),
        ),
        in_specs=[sm, sm, sm, sm, vm, vm, vm],
        out_specs=(vm, vm),
        scratch_shapes=[
            pltpu.VMEM((chans, stations, 48), jnp.bfloat16),
            pltpu.VMEM((steps, 8, CHUNK), jnp.float32),
        ]
        + [pltpu.VMEM((side, side), jnp.float32)] * count
        + [pltpu.VMEM((side, side), jnp.bfloat16)] * count
        + [pltpu.VMEM((NB, two, CHUNK), jnp.bfloat16)] * (chans * steps),
        compiler_params=pltpu.CompilerParams(vmem_limit_bytes=48 * 2**20),
        name="visibility",
    )(ib, jb, dest, ratio, uvw, d, ref)


def slot_tables(own_pairs):
    starts = np.asarray([i * NB - i * (i - 1) // 2 for i in range(NB)], np.int32)
    row = jnp.sum((own_pairs[:, None] >= jnp.asarray(starts)[None, :]).astype(jnp.int32), axis=1) - 1
    col = own_pairs - (row * NB - row * (row - 1) // 2) + row
    return row, col


def reference_blocks(observed, on_diag, side):
    chans, slots, _ = observed.shape
    shaped = observed.reshape(chans, slots, 2, side, side)
    above = jnp.asarray(np.arange(side)[:, None] < np.arange(side)[None, :])
    part = jnp.where(above, shaped, 0.0)
    turned = jnp.swapaxes(part, -1, -2)
    herm = jnp.stack([part[:, :, 0] + turned[:, :, 0], part[:, :, 1] - turned[:, :, 1]], axis=2)
    out = jnp.where(on_diag[None, :, None, None, None], herm, shaped)
    return out.reshape(chans, slots, 2 * side, side)


def swap_perm(count, k):
    return [(i, i ^ k) for i in range(count)]


def gather_components(own, count):
    me = lax.axis_index("comp")
    parts = {0: own}
    for k in (1, 2, 3):
        parts[k] = lax.ppermute(own, "comp", swap_perm(count, k))
    low = jnp.stack([parts[k] for k in range(4)], axis=0)
    rounds = {0: low}
    for k in (4, 8, 12):
        rounds[k] = lax.ppermute(low, "comp", swap_perm(count, k))
    return jnp.stack([rounds[k] for k in (0, 4, 8, 12)], axis=0)


def body(station_uvw, directions, flux_ref, spectral_index, channel_index, slot_pair, observed):
    comp_count = lax.axis_size("comp")
    group_count = lax.axis_size("freq")
    stations = station_uvw.shape[1]
    side = stations // NB
    chans = channel_index.shape[0]
    own_slots = observed.shape[1]
    per_block = directions.shape[1]
    total = per_block * comp_count
    scale = 1.0 / math.sqrt(total)
    me = lax.axis_index("comp")
    ratios = 1.0 + channel_index.astype(jnp.float32) / 4096.0

    blank = jnp.zeros((3, per_block), jnp.float32)
    own = jnp.concatenate(
        [directions, blank[:1], flux_ref[None], spectral_index[None], blank], axis=0
    )
    d = gather_components(own, comp_count).reshape(comp_count, 8, per_block)
    dest = me ^ jnp.arange(comp_count, dtype=jnp.int32)
    ratio = jnp.stack([ratios, jnp.log2(ratios)], axis=0)

    own_pairs = lax.dynamic_slice_in_dim(slot_pair, me * own_slots, own_slots)
    ib, jb = slot_tables(own_pairs)
    ref = reference_blocks(observed, ib == jb, side)
    res, sent = device_kernel(ib, jb, dest, ratio, station_uvw, d, ref, group_count)
    residual = res.reshape(chans, own_slots, 2 * side * side)
    got = lax.all_to_all(sent, ("comp", "freq"), 0, 0, tiled=True)
    flux_grad = jnp.sum(got, axis=(0, 1)) / (flux_ref * (scale * stations * chans * group_count))
    return residual, flux_grad


def solution(mesh):
    in_specs = (P(), P(None, "comp"), P("comp"), P("comp"), P("freq"), P(), P("freq", "comp", None))
    out_specs = (P("freq", "comp", None), P("comp"))
    return jax.shard_map(body, mesh=mesh, in_specs=in_specs, out_specs=out_specs, check_vma=False)
```

```python
import math

import jax
import jax.numpy as jnp
import numpy as np
from jax import lax
from jax.experimental import pallas as pl
from jax.experimental.pallas import tpu as pltpu
from jax.sharding import PartitionSpec as P

NB = 32
GROUP = 8
CHUNK = 512
ROWS = 256
SIN_COEF = tuple(
    k * (1.0 - 2.0e-6) for k in (3.14158202, -5.16714276, 2.54189867, -0.55463514)
)


def pieces(x):
    hi = x.astype(jnp.bfloat16).astype(jnp.float32)
    rest = x - hi
    mid = rest.astype(jnp.bfloat16).astype(jnp.float32)
    low = (rest - mid).astype(jnp.bfloat16).astype(jnp.float32)
    return hi, mid, low


def weave(*parts):
    parts = list(parts)
    while parts:
        for part in list(parts):
            if next(part, parts) is parts:
                parts.remove(part)


def kernel(
    ib_ref, jb_ref, ratio_ref, uvw_ref, d_ref, ref_ref, res_ref, sent_ref, lhs_ref, acc_ref, *rest
):
    chans, slots, two, side = ref_ref.shape
    blocks, _, width = d_ref.shape
    stations = uvw_ref.shape[1]
    copies = sent_ref.shape[0] // blocks
    comps = blocks * width
    scale = 1.0 / math.sqrt(comps)
    steps = comps // CHUNK
    per = CHUNK // width
    groups = [(g, min(GROUP, slots - g)) for g in range(0, slots, GROUP)]
    count_g = len(groups)
    p_refs = rest[: chans * count_g]
    g_refs = rest[chans * count_g : 2 * chans * count_g]
    q_refs = rest[2 * chans * count_g :]

    def stack(q_ref, ref, first, count):
        return jnp.concatenate([q_ref[ref[first + k]] for k in range(count)], axis=0)

    def stations_of(ch):
        uvw = jnp.concatenate(
            [uvw_ref[...] * ratio_ref[0, ch], jnp.zeros((5, stations), jnp.float32)], axis=0
        )
        hi, mid, low = pieces(uvw)
        rows = jnp.concatenate([hi, hi, hi, mid, mid, low], axis=0)
        lhs_ref[ch] = rows.T.astype(jnp.bfloat16)

    def phasors(ch, step):
        q_ref = q_refs[ch * steps + step]
        d = jnp.concatenate([d_ref[step * per + k] for k in range(per)], axis=1)
        l_part, m_part = d[0:1], d[1:2]
        w_term = jnp.sqrt(1.0 - l_part * l_part - m_part * m_part) - 1.0
        row = lax.broadcasted_iota(jnp.int32, d.shape, 0)
        hi, mid, low = pieces(jnp.where(row == 2, w_term, d))
        rhs = jnp.concatenate([hi, mid, low, hi, mid, hi], axis=0).astype(jnp.bfloat16)
        gain = jnp.sqrt(d[3:4] * jnp.exp2(d[4:5] * ratio_ref[1, ch]) * scale)
        root = jnp.sqrt(2.0 * gain)
        coef = [jnp.broadcast_to(-k * root, (8, CHUNK))[None] for k in SIN_COEF]
        gain1 = jnp.broadcast_to(gain, (8, CHUNK))[None]
        gain2 = 2.0 * gain1
        for r in range(0, stations, ROWS):
            t = jnp.dot(
                lhs_ref[ch, r : r + ROWS], rhs, preferred_element_type=jnp.float32
            ).reshape(ROWS // 8, 8, CHUNK)
            x = t - jnp.round(t)
            z = x * x
            poly = coef[-1]
            for k in coef[-2::-1]:
                poly = k + z * poly
            s = x * poly
            y = s * s
            w = gain2 - y
            co = w * lax.rsqrt(w)
            im = (s * co).astype(jnp.bfloat16).reshape(ROWS // side, side, CHUNK)
            re = (gain1 - y).astype(jnp.bfloat16).reshape(ROWS // side, side, CHUNK)
            b = r // side
            q_ref[b : b + ROWS // side, 0:side] = re
            q_ref[b : b + ROWS // side, side:two] = im
            yield

    def model(ch, step):
        q_ref = q_refs[ch * steps + step]
        for gi, (first, count) in enumerate(groups):
            size = count * two
            part = lax.dot_general(
                stack(q_ref, ib_ref, first, count),
                stack(q_ref, jb_ref, first, count),
                (((1,), (1,)), ((), ())),
                preferred_element_type=jnp.float32,
            )
            p_ref = p_refs[ch * count_g + gi]
            if step == 0:
                p_ref[0:size, 0:size] = part
            else:
                p_ref[0:size, 0:size] += part
            yield

    def residuals(ch):
        lane = lax.broadcasted_iota(jnp.int32, (two, 128), 1)
        row = lax.broadcasted_iota(jnp.int32, (two, 128), 0)
        top = row < side
        auto = jnp.where(top, row, row - side) == lane
        pad = jnp.zeros((two, 128 - side), jnp.float32)
        for gi, (first, count) in enumerate(groups):
            p_ref = p_refs[ch * count_g + gi]
            g_ref = g_refs[ch * count_g + gi]
            g_ref[...] = jnp.zeros(g_ref.shape, g_ref.dtype)
            for k in range(count):
                base = k * two
                window = (base // 128) * 128
                shift = base % 128
                blk = p_ref[base : base + two, window : window + 128]
                if shift:
                    blk = pltpu.roll(blk, 128 - shift, 1)
                swap = jnp.concatenate([blk[side:], -blk[:side]], axis=0)
                swap = pltpu.roll(swap, 128 - side, 1)
                diag = ib_ref[first + k] == jb_ref[first + k]
                seen = jnp.concatenate([ref_ref[ch, first + k], pad], axis=1)
                res = blk + swap - seen
                res = jnp.where((lane >= side) | (auto & diag), 0.0, res)
                res_ref[ch, first + k] = res[:, :side]
                scaled = res * jnp.where(diag, 1.0, 2.0)
                other = jnp.concatenate([-scaled[side:], scaled[:side]], axis=0)
                full = scaled + pltpu.roll(other, side, 1)
                if shift:
                    full = pltpu.roll(full, shift, 1)
                g_ref[base : base + two, window : window + 128] = full.astype(jnp.bfloat16)

    def gradient(ch, step):
        q_ref = q_refs[ch * steps + step]
        acc = jnp.zeros((8, CHUNK), jnp.float32)
        for gi, (first, count) in enumerate(groups):
            size = count * two
            m = jnp.dot(
                g_refs[ch * count_g + gi][0:size, 0:size],
                stack(q_ref, jb_ref, first, count),
                preferred_element_type=jnp.float32,
            )
            m = stack(q_ref, ib_ref, first, count).astype(jnp.float32) * m
            acc = acc + jnp.sum(m.reshape(size // 8, 8, CHUNK), axis=0)
            yield
        if ch > 0:
            acc = acc + acc_ref[step]
        if ch < chans - 1:
            acc_ref[step] = acc
            return
        total = jnp.sum(acc, axis=0, keepdims=True)
        for k in range(per):
            line = total[:, k * width : (k + 1) * width]
            first = (step * per + k) * copies
            sent_ref[first : first + copies] = jnp.broadcast_to(line[None], (copies, 1, width))

    for ch in range(chans):
        stations_of(ch)
    for ch in range(chans):
        for step in range(steps):
            if step > 0:
                beside = [model(ch, step - 1)]
                if ch > 0:
                    beside.append(gradient(ch - 1, step - 1))
                weave(phasors(ch, step), *beside)
            elif ch > 0:
                weave(phasors(ch, step), model(ch - 1, steps - 1))
                residuals(ch - 1)
            else:
                weave(phasors(ch, step))
    last = chans - 1
    if last > 0:
        weave(model(last, steps - 1), gradient(last - 1, steps - 1))
    else:
        weave(model(last, steps - 1))
    residuals(last)
    for step in range(steps):
        weave(gradient(last, step))


def device_kernel(ib, jb, ratio, uvw, d, ref, copies):
    chans, slots, two, _ = ref.shape
    blocks, _, width = d.shape
    stations = uvw.shape[1]
    steps = blocks * width // CHUNK
    vm = pl.BlockSpec(memory_space=pltpu.VMEM)
    sm = pl.BlockSpec(memory_space=pltpu.SMEM)
    side = GROUP * two
    count = chans * -(-slots // GROUP)
    return pl.pallas_call(
        kernel,
        out_shape=(
            jax.ShapeDtypeStruct(ref.shape, jnp.float32),
            jax.ShapeDtypeStruct((blocks * copies, 1, width), jnp.float32),
        ),
        in_specs=[sm, sm, sm, vm, vm, vm],
        out_specs=(vm, vm),
        scratch_shapes=[
            pltpu.VMEM((chans, stations, 48), jnp.bfloat16),
            pltpu.VMEM((steps, 8, CHUNK), jnp.float32),
        ]
        + [pltpu.VMEM((side, side), jnp.float32)] * count
        + [pltpu.VMEM((side, side), jnp.bfloat16)] * count
        + [pltpu.VMEM((NB, two, CHUNK), jnp.bfloat16)] * (chans * steps),
        compiler_params=pltpu.CompilerParams(vmem_limit_bytes=48 * 2**20),
        name="visibility",
    )(ib, jb, ratio, uvw, d, ref)


def slot_tables(own_pairs):
    starts = np.asarray([i * NB - i * (i - 1) // 2 for i in range(NB)], np.int32)
    row = jnp.sum((own_pairs[:, None] >= jnp.asarray(starts)[None, :]).astype(jnp.int32), axis=1) - 1
    col = own_pairs - (row * NB - row * (row - 1) // 2) + row
    return row, col


def reference_blocks(observed, on_diag, side):
    chans, slots, _ = observed.shape
    shaped = observed.reshape(chans, slots, 2, side, side)
    above = jnp.asarray(np.arange(side)[:, None] < np.arange(side)[None, :])
    part = jnp.where(above, shaped, 0.0)
    turned = jnp.swapaxes(part, -1, -2)
    herm = jnp.stack([part[:, :, 0] + turned[:, :, 0], part[:, :, 1] - turned[:, :, 1]], axis=2)
    out = jnp.where(on_diag[None, :, None, None, None], herm, shaped)
    return out.reshape(chans, slots, 2 * side, side)


def body(station_uvw, directions, flux_ref, spectral_index, channel_index, slot_pair, observed):
    comp_count = lax.axis_size("comp")
    group_count = lax.axis_size("freq")
    stations = station_uvw.shape[1]
    side = stations // NB
    chans = channel_index.shape[0]
    own_slots = observed.shape[1]
    per_block = directions.shape[1]
    total = per_block * comp_count
    scale = 1.0 / math.sqrt(total)
    me = lax.axis_index("comp")
    ratios = 1.0 + channel_index.astype(jnp.float32) / 4096.0

    rows = [directions, jnp.zeros((1, per_block), jnp.float32), flux_ref[None], spectral_index[None]]
    rows.append(jnp.zeros((8 - 5, per_block), jnp.float32))
    own = jnp.concatenate(
        [jnp.broadcast_to(row[None], (comp_count,) + row.shape) for row in rows], axis=1
    )
    d = lax.all_to_all(own, "comp", 0, 0, tiled=True)
    ratio = jnp.stack([ratios, jnp.log2(ratios)], axis=0)

    own_pairs = lax.dynamic_slice_in_dim(slot_pair, me * own_slots, own_slots)
    ib, jb = slot_tables(own_pairs)
    ref = reference_blocks(observed, ib == jb, side)
    res, sent = device_kernel(ib, jb, ratio, station_uvw, d, ref, group_count)
    residual = res.reshape(chans, own_slots, 2 * side * side)
    got = lax.all_to_all(sent, ("comp", "freq"), 0, 0, tiled=True)
    flux_grad = jnp.sum(got, axis=(0, 1)) / (flux_ref * (scale * stations * chans * group_count))
    return residual, flux_grad


def solution(mesh):
    in_specs = (P(), P(None, "comp"), P("comp"), P("comp"), P("freq"), P(), P("freq", "comp", None))
    out_specs = (P("freq", "comp", None), P("comp"))
    return jax.shard_map(body, mesh=mesh, in_specs=in_specs, out_specs=out_specs, check_vma=False)
```

```python
import math

import jax
import jax.numpy as jnp
import numpy as np
from jax import lax
from jax.experimental import pallas as pl
from jax.experimental.pallas import tpu as pltpu
from jax.sharding import PartitionSpec as P

NB = 32
GROUP = 8
CHUNK = 512
ROWS = 256
SIN_COEF = tuple(
    k * (1.0 - 2.0e-6) for k in (3.14158202, -5.16714276, 2.54189867, -0.55463514)
)


def pieces(x):
    hi = x.astype(jnp.bfloat16).astype(jnp.float32)
    rest = x - hi
    mid = rest.astype(jnp.bfloat16).astype(jnp.float32)
    low = (rest - mid).astype(jnp.bfloat16).astype(jnp.float32)
    return hi, mid, low


def weave(*parts):
    parts = list(parts)
    while parts:
        for part in list(parts):
            if next(part, parts) is parts:
                parts.remove(part)


def kernel(
    ib_ref, jb_ref, ratio_ref, uvw_ref, d_ref, ref_ref, res_ref, sent_ref, lhs_ref, acc_ref, *rest
):
    chans, slots, two, side = ref_ref.shape
    blocks, _, width = d_ref.shape
    stations = uvw_ref.shape[1]
    copies = sent_ref.shape[0] // blocks
    comps = blocks * width
    scale = 1.0 / math.sqrt(comps)
    steps = comps // CHUNK
    per = CHUNK // width
    groups = [(g, min(GROUP, slots - g)) for g in range(0, slots, GROUP)]
    count_g = len(groups)
    p_refs = rest[: chans * count_g]
    g_refs = rest[chans * count_g : 2 * chans * count_g]
    q_refs = rest[2 * chans * count_g :]

    def stack(q_ref, ref, first, count):
        return jnp.concatenate([q_ref[ref[first + k]] for k in range(count)], axis=0)

    def stations_of(ch):
        uvw = jnp.concatenate(
            [uvw_ref[...] * ratio_ref[0, ch], jnp.zeros((5, stations), jnp.float32)], axis=0
        )
        hi, mid, low = pieces(uvw)
        rows = jnp.concatenate([hi, hi, hi, mid, mid, low], axis=0)
        lhs_ref[ch] = rows.T.astype(jnp.bfloat16)

    def phasors(ch, step):
        q_ref = q_refs[ch * steps + step]
        d = jnp.concatenate([d_ref[step * per + k] for k in range(per)], axis=1)
        l_part, m_part = d[0:1], d[1:2]
        w_term = jnp.sqrt(1.0 - l_part * l_part - m_part * m_part) - 1.0
        row = lax.broadcasted_iota(jnp.int32, d.shape, 0)
        hi, mid, low = pieces(jnp.where(row == 2, w_term, d))
        rhs = jnp.concatenate([hi, mid, low, hi, mid, hi], axis=0).astype(jnp.bfloat16)
        gain = jnp.sqrt(d[3:4] * jnp.exp2(d[4:5] * ratio_ref[1, ch]) * scale)
        root = jnp.sqrt(2.0 * gain)
        coef = [jnp.broadcast_to(-k * root, (8, CHUNK))[None] for k in SIN_COEF]
        gain1 = jnp.broadcast_to(gain, (8, CHUNK))[None]
        gain2 = 2.0 * gain1
        for r in range(0, stations, ROWS):
            t = jnp.dot(
                lhs_ref[ch, r : r + ROWS], rhs, preferred_element_type=jnp.float32
            ).reshape(ROWS // 8, 8, CHUNK)
            x = t - jnp.round(t)
            z = x * x
            poly = coef[-1]
            for k in coef[-2::-1]:
                poly = k + z * poly
            s = x * poly
            y = s * s
            w = gain2 - y
            co = w * lax.rsqrt(w)
            im = (s * co).astype(jnp.bfloat16).reshape(ROWS // side, side, CHUNK)
            re = (gain1 - y).astype(jnp.bfloat16).reshape(ROWS // side, side, CHUNK)
            b = r // side
            q_ref[b : b + ROWS // side, 0:side] = re
            q_ref[b : b + ROWS // side, side:two] = im
            yield

    def model(ch, step):
        q_ref = q_refs[ch * steps + step]
        for gi, (first, count) in enumerate(groups):
            size = count * two
            part = lax.dot_general(
                stack(q_ref, ib_ref, first, count),
                stack(q_ref, jb_ref, first, count),
                (((1,), (1,)), ((), ())),
                preferred_element_type=jnp.float32,
            )
            p_ref = p_refs[ch * count_g + gi]
            if step == 0:
                p_ref[0:size, 0:size] = part
            else:
                p_ref[0:size, 0:size] += part
            yield

    def residuals(ch):
        lane = lax.broadcasted_iota(jnp.int32, (two, 128), 1)
        row = lax.broadcasted_iota(jnp.int32, (two, 128), 0)
        top = row < side
        auto = jnp.where(top, row, row - side) == lane
        pad = jnp.zeros((two, 128 - side), jnp.float32)
        for gi, (first, count) in enumerate(groups):
            p_ref = p_refs[ch * count_g + gi]
            g_ref = g_refs[ch * count_g + gi]
            g_ref[...] = jnp.zeros(g_ref.shape, g_ref.dtype)
            for k in range(count):
                base = k * two
                window = (base // 128) * 128
                shift = base % 128
                blk = p_ref[base : base + two, window : window + 128]
                if shift:
                    blk = pltpu.roll(blk, 128 - shift, 1)
                swap = jnp.concatenate([blk[side:], -blk[:side]], axis=0)
                swap = pltpu.roll(swap, 128 - side, 1)
                diag = ib_ref[first + k] == jb_ref[first + k]
                seen = jnp.concatenate([ref_ref[ch, first + k], pad], axis=1)
                res = blk + swap - seen
                res = jnp.where((lane >= side) | (auto & diag), 0.0, res)
                res_ref[ch, first + k] = res[:, :side]
                scaled = res * jnp.where(diag, 1.0, 2.0)
                other = jnp.concatenate([-scaled[side:], scaled[:side]], axis=0)
                full = scaled + pltpu.roll(other, side, 1)
                if shift:
                    full = pltpu.roll(full, shift, 1)
                g_ref[base : base + two, window : window + 128] = full.astype(jnp.bfloat16)

    def gradient(ch, step):
        q_ref = q_refs[ch * steps + step]
        acc = jnp.zeros((8, CHUNK), jnp.float32)
        for gi, (first, count) in enumerate(groups):
            size = count * two
            m = jnp.dot(
                g_refs[ch * count_g + gi][0:size, 0:size],
                stack(q_ref, jb_ref, first, count),
                preferred_element_type=jnp.float32,
            )
            m = stack(q_ref, ib_ref, first, count) * m.astype(jnp.bfloat16)
            m = m.reshape(size // 32, 2, 16, CHUNK)
            m = (m[:, 0] + m[:, 1]).astype(jnp.float32)
            acc = acc + jnp.sum(m.reshape(size // 16, 8, CHUNK), axis=0)
            yield
        if ch > 0:
            acc = acc + acc_ref[step]
        if ch < chans - 1:
            acc_ref[step] = acc
            return
        flux = jnp.concatenate([d_ref[step * per + k][3:4] for k in range(per)], axis=1)
        total = jnp.sum(acc, axis=0, keepdims=True) / (flux * (scale * stations * chans * copies))
        for k in range(per):
            line = total[:, k * width : (k + 1) * width]
            first = (step * per + k) * copies
            sent_ref[first : first + copies] = jnp.broadcast_to(line[None], (copies, 1, width))

    for ch in range(chans):
        stations_of(ch)
    for ch in range(chans):
        for step in range(steps):
            if step > 0:
                beside = [model(ch, step - 1)]
                if ch > 0:
                    beside.append(gradient(ch - 1, step - 1))
                weave(phasors(ch, step), *beside)
            elif ch > 0:
                weave(phasors(ch, step), model(ch - 1, steps - 1))
                residuals(ch - 1)
            else:
                weave(phasors(ch, step))
    last = chans - 1
    if last > 0:
        weave(model(last, steps - 1), gradient(last - 1, steps - 1))
    else:
        weave(model(last, steps - 1))
    residuals(last)
    for step in range(steps):
        weave(gradient(last, step))


def device_kernel(ib, jb, ratio, uvw, d, ref, copies):
    chans, slots, two, _ = ref.shape
    blocks, _, width = d.shape
    stations = uvw.shape[1]
    steps = blocks * width // CHUNK
    vm = pl.BlockSpec(memory_space=pltpu.VMEM)
    sm = pl.BlockSpec(memory_space=pltpu.SMEM)
    side = GROUP * two
    count = chans * -(-slots // GROUP)
    return pl.pallas_call(
        kernel,
        out_shape=(
            jax.ShapeDtypeStruct(ref.shape, jnp.float32),
            jax.ShapeDtypeStruct((blocks * copies, 1, width), jnp.float32),
        ),
        in_specs=[sm, sm, sm, vm, vm, vm],
        out_specs=(vm, vm),
        scratch_shapes=[
            pltpu.VMEM((chans, stations, 48), jnp.bfloat16),
            pltpu.VMEM((steps, 8, CHUNK), jnp.float32),
        ]
        + [pltpu.VMEM((side, side), jnp.float32)] * count
        + [pltpu.VMEM((side, side), jnp.bfloat16)] * count
        + [pltpu.VMEM((NB, two, CHUNK), jnp.bfloat16)] * (chans * steps),
        compiler_params=pltpu.CompilerParams(vmem_limit_bytes=48 * 2**20),
        name="visibility",
    )(ib, jb, ratio, uvw, d, ref)


def slot_tables(own_pairs):
    starts = np.asarray([i * NB - i * (i - 1) // 2 for i in range(NB)], np.int32)
    row = jnp.sum((own_pairs[:, None] >= jnp.asarray(starts)[None, :]).astype(jnp.int32), axis=1) - 1
    col = own_pairs - (row * NB - row * (row - 1) // 2) + row
    return row, col


def reference_blocks(observed, on_diag, side):
    chans, slots, _ = observed.shape
    shaped = observed.reshape(chans, slots, 2, side, side)
    above = jnp.asarray(np.arange(side)[:, None] < np.arange(side)[None, :])
    part = jnp.where(above, shaped, 0.0)
    turned = jnp.swapaxes(part, -1, -2)
    herm = jnp.stack([part[:, :, 0] + turned[:, :, 0], part[:, :, 1] - turned[:, :, 1]], axis=2)
    out = jnp.where(on_diag[None, :, None, None, None], herm, shaped)
    return out.reshape(chans, slots, 2 * side, side)


def body(station_uvw, directions, flux_ref, spectral_index, channel_index, slot_pair, observed):
    comp_count = lax.axis_size("comp")
    group_count = lax.axis_size("freq")
    stations = station_uvw.shape[1]
    side = stations // NB
    chans = channel_index.shape[0]
    own_slots = observed.shape[1]
    per_block = directions.shape[1]
    me = lax.axis_index("comp")
    ratios = 1.0 + channel_index.astype(jnp.float32) / 4096.0

    own = jnp.concatenate(
        [
            directions,
            jnp.zeros((1, per_block), jnp.float32),
            flux_ref[None],
            spectral_index[None],
            jnp.zeros((3, per_block), jnp.float32),
        ],
        axis=0,
    )
    copies = lax.optimization_barrier(jnp.broadcast_to(own[None], (comp_count,) + own.shape))
    d = lax.all_to_all(copies, "comp", 0, 0, tiled=True)
    ratio = jnp.stack([ratios, jnp.log2(ratios)], axis=0)

    own_pairs = lax.dynamic_slice_in_dim(slot_pair, me * own_slots, own_slots)
    ib, jb = slot_tables(own_pairs)
    ref = reference_blocks(observed, ib == jb, side)
    res, sent = device_kernel(ib, jb, ratio, station_uvw, d, ref, group_count)
    residual = res.reshape(chans, own_slots, 2 * side * side)
    got = lax.all_to_all(sent, ("comp", "freq"), 0, 0, tiled=True)
    flux_grad = jnp.sum(got, axis=(0, 1))
    return residual, flux_grad


def solution(mesh):
    in_specs = (P(), P(None, "comp"), P("comp"), P("comp"), P("freq"), P(), P("freq", "comp", None))
    out_specs = (P("freq", "comp", None), P("comp"))
    return jax.shard_map(body, mesh=mesh, in_specs=in_specs, out_specs=out_specs, check_vma=False)
```

```python
import math

import jax
import jax.numpy as jnp
import numpy as np
from jax import lax
from jax.experimental import pallas as pl
from jax.experimental.pallas import tpu as pltpu
from jax.sharding import PartitionSpec as P

NB = 32
GROUP = 8
CHUNK = 512
ROWS = 256
SIN_COEF = tuple(
    k * (1.0 - 2.0e-6) for k in (3.14158202, -5.16714276, 2.54189867, -0.55463514)
)


def pieces(x):
    hi = x.astype(jnp.bfloat16).astype(jnp.float32)
    rest = x - hi
    mid = rest.astype(jnp.bfloat16).astype(jnp.float32)
    low = (rest - mid).astype(jnp.bfloat16).astype(jnp.float32)
    return hi, mid, low


def weave(*parts):
    parts = list(parts)
    while parts:
        for part in list(parts):
            if next(part, parts) is parts:
                parts.remove(part)


def kernel(
    ib_ref, jb_ref, ratio_ref, uvw_ref, d_ref, ref_ref, res_ref, sent_ref, lhs_ref, acc_ref, *rest
):
    chans, slots, two, side = ref_ref.shape
    blocks, _, width = d_ref.shape
    stations = uvw_ref.shape[1]
    copies = sent_ref.shape[0] // blocks
    comps = blocks * width
    scale = 1.0 / math.sqrt(comps)
    steps = comps // CHUNK
    per = CHUNK // width
    groups = [(g, min(GROUP, slots - g)) for g in range(0, slots, GROUP)]
    count_g = len(groups)
    p_refs = rest[: chans * count_g]
    g_refs = rest[chans * count_g : 2 * chans * count_g]
    q_refs = rest[2 * chans * count_g :]

    def stack(q_ref, ref, first, count):
        return jnp.concatenate([q_ref[ref[first + k]] for k in range(count)], axis=0)

    def stations_of(ch):
        uvw = jnp.concatenate(
            [uvw_ref[...] * ratio_ref[0, ch], jnp.zeros((5, stations), jnp.float32)], axis=0
        )
        hi, mid, low = pieces(uvw)
        rows = jnp.concatenate([hi, hi, hi, mid, mid, low], axis=0)
        lhs_ref[ch] = rows.T.astype(jnp.bfloat16)

    def phasors(ch, step):
        q_ref = q_refs[ch * steps + step]
        d = jnp.concatenate([d_ref[step * per + k] for k in range(per)], axis=1)
        l_part, m_part = d[0:1], d[1:2]
        w_term = jnp.sqrt(1.0 - l_part * l_part - m_part * m_part) - 1.0
        blank = jnp.zeros((5, CHUNK), jnp.float32)
        hi, mid, low = pieces(jnp.concatenate([l_part, m_part, w_term, blank], axis=0))
        rhs = jnp.concatenate([hi, mid, low, hi, mid, hi], axis=0).astype(jnp.bfloat16)
        gain = jnp.sqrt(d[2:3] * jnp.exp2(d[3:4] * ratio_ref[1, ch]) * scale)
        root = jnp.sqrt(2.0 * gain)
        coef = [jnp.broadcast_to(-k * root, (8, CHUNK))[None] for k in SIN_COEF]
        gain1 = jnp.broadcast_to(gain, (8, CHUNK))[None]
        gain2 = 2.0 * gain1
        for r in range(0, stations, ROWS):
            t = jnp.dot(
                lhs_ref[ch, r : r + ROWS], rhs, preferred_element_type=jnp.float32
            ).reshape(ROWS // 8, 8, CHUNK)
            x = t - jnp.round(t)
            z = x * x
            poly = coef[-1]
            for k in coef[-2::-1]:
                poly = k + z * poly
            s = x * poly
            y = s * s
            w = gain2 - y
            co = w * lax.rsqrt(w)
            im = (s * co).astype(jnp.bfloat16).reshape(ROWS // side, side, CHUNK)
            re = (gain1 - y).astype(jnp.bfloat16).reshape(ROWS // side, side, CHUNK)
            b = r // side
            q_ref[b : b + ROWS // side, 0:side] = re
            q_ref[b : b + ROWS // side, side:two] = im
            yield

    def model(ch, step):
        q_ref = q_refs[ch * steps + step]
        for gi, (first, count) in enumerate(groups):
            size = count * two
            part = lax.dot_general(
                stack(q_ref, ib_ref, first, count),
                stack(q_ref, jb_ref, first, count),
                (((1,), (1,)), ((), ())),
                preferred_element_type=jnp.float32,
            )
            p_ref = p_refs[ch * count_g + gi]
            if step == 0:
                p_ref[0:size, 0:size] = part
            else:
                p_ref[0:size, 0:size] += part
            yield

    def residuals(ch):
        lane = lax.broadcasted_iota(jnp.int32, (two, 128), 1)
        row = lax.broadcasted_iota(jnp.int32, (two, 128), 0)
        top = row < side
        auto = jnp.where(top, row, row - side) == lane
        pad = jnp.zeros((two, 128 - side), jnp.float32)
        for gi, (first, count) in enumerate(groups):
            p_ref = p_refs[ch * count_g + gi]
            g_ref = g_refs[ch * count_g + gi]
            g_ref[...] = jnp.zeros(g_ref.shape, g_ref.dtype)
            for k in range(count):
                base = k * two
                window = (base // 128) * 128
                shift = base % 128
                blk = p_ref[base : base + two, window : window + 128]
                if shift:
                    blk = pltpu.roll(blk, 128 - shift, 1)
                swap = jnp.concatenate([blk[side:], -blk[:side]], axis=0)
                swap = pltpu.roll(swap, 128 - side, 1)
                diag = ib_ref[first + k] == jb_ref[first + k]
                seen = jnp.concatenate([ref_ref[ch, first + k], pad], axis=1)
                res = blk + swap - seen
                res = jnp.where((lane >= side) | (auto & diag), 0.0, res)
                res_ref[ch, first + k] = res[:, :side]
                scaled = res * jnp.where(diag, 1.0, 2.0)
                other = jnp.concatenate([-scaled[side:], scaled[:side]], axis=0)
                full = scaled + pltpu.roll(other, side, 1)
                if shift:
                    full = pltpu.roll(full, shift, 1)
                g_ref[base : base + two, window : window + 128] = full.astype(jnp.bfloat16)

    def gradient(ch, step):
        q_ref = q_refs[ch * steps + step]
        acc = jnp.zeros((8, CHUNK), jnp.float32)
        for gi, (first, count) in enumerate(groups):
            size = count * two
            m = jnp.dot(
                g_refs[ch * count_g + gi][0:size, 0:size],
                stack(q_ref, jb_ref, first, count),
                preferred_element_type=jnp.float32,
            )
            m = stack(q_ref, ib_ref, first, count) * m.astype(jnp.bfloat16)
            m = m.reshape(size // 32, 2, 16, CHUNK)
            m = (m[:, 0] + m[:, 1]).astype(jnp.float32)
            acc = acc + jnp.sum(m.reshape(size // 16, 8, CHUNK), axis=0)
            yield
        if ch > 0:
            acc = acc + acc_ref[step]
        if ch < chans - 1:
            acc_ref[step] = acc
            return
        flux = jnp.concatenate([d_ref[step * per + k][2:3] for k in range(per)], axis=1)
        total = jnp.sum(acc, axis=0, keepdims=True) / (flux * (scale * stations * chans * copies))
        for k in range(per):
            line = total[:, k * width : (k + 1) * width]
            first = (step * per + k) * copies
            sent_ref[first : first + copies] = jnp.broadcast_to(line[None], (copies, 1, width))

    for ch in range(chans):
        stations_of(ch)
        for step in range(steps):
            if step > 0:
                beside = [model(ch, step - 1)]
                if ch > 0:
                    beside.append(gradient(ch - 1, step - 1))
                weave(phasors(ch, step), *beside)
            elif ch > 0:
                weave(phasors(ch, step), model(ch - 1, steps - 1))
                residuals(ch - 1)
            else:
                weave(phasors(ch, step))
    last = chans - 1
    if last > 0:
        weave(model(last, steps - 1), gradient(last - 1, steps - 1))
    else:
        weave(model(last, steps - 1))
    residuals(last)
    for step in range(steps):
        weave(gradient(last, step))


def device_kernel(ib, jb, ratio, uvw, d, ref, copies):
    chans, slots, two, _ = ref.shape
    blocks, _, width = d.shape
    stations = uvw.shape[1]
    steps = blocks * width // CHUNK
    vm = pl.BlockSpec(memory_space=pltpu.VMEM)
    sm = pl.BlockSpec(memory_space=pltpu.SMEM)
    side = GROUP * two
    count = chans * -(-slots // GROUP)
    return pl.pallas_call(
        kernel,
        out_shape=(
            jax.ShapeDtypeStruct(ref.shape, jnp.float32),
            jax.ShapeDtypeStruct((blocks * copies, 1, width), jnp.float32),
        ),
        in_specs=[sm, sm, sm, vm, vm, vm],
        out_specs=(vm, vm),
        scratch_shapes=[
            pltpu.VMEM((chans, stations, 48), jnp.bfloat16),
            pltpu.VMEM((steps, 8, CHUNK), jnp.float32),
        ]
        + [pltpu.VMEM((side, side), jnp.float32)] * count
        + [pltpu.VMEM((side, side), jnp.bfloat16)] * count
        + [pltpu.VMEM((NB, two, CHUNK), jnp.bfloat16)] * (chans * steps),
        compiler_params=pltpu.CompilerParams(vmem_limit_bytes=48 * 2**20),
        name="visibility",
    )(ib, jb, ratio, uvw, d, ref)


def slot_tables(own_pairs):
    starts = np.asarray([i * NB - i * (i - 1) // 2 for i in range(NB)], np.int32)
    row = jnp.sum((own_pairs[:, None] >= jnp.asarray(starts)[None, :]).astype(jnp.int32), axis=1) - 1
    col = own_pairs - (row * NB - row * (row - 1) // 2) + row
    return row, col


def reference_blocks(observed, on_diag, side):
    chans, slots, _ = observed.shape
    shaped = observed.reshape(chans, slots, 2, side, side)
    above = jnp.asarray(np.arange(side)[:, None] < np.arange(side)[None, :])
    part = jnp.where(above, shaped, 0.0)
    turned = jnp.swapaxes(part, -1, -2)
    herm = jnp.stack([part[:, :, 0] + turned[:, :, 0], part[:, :, 1] - turned[:, :, 1]], axis=2)
    out = jnp.where(on_diag[None, :, None, None, None], herm, shaped)
    return out.reshape(chans, slots, 2 * side, side)


def body(station_uvw, directions, flux_ref, spectral_index, channel_index, slot_pair, observed):
    comp_count = lax.axis_size("comp")
    group_count = lax.axis_size("freq")
    stations = station_uvw.shape[1]
    side = stations // NB
    chans = channel_index.shape[0]
    own_slots = observed.shape[1]
    per_block = directions.shape[1]
    me = lax.axis_index("comp")
    ratios = 1.0 + channel_index.astype(jnp.float32) / 4096.0

    own = jnp.concatenate(
        [
            directions,
            flux_ref[None],
            spectral_index[None],
        ],
        axis=0,
    )
    copies = lax.optimization_barrier(jnp.broadcast_to(own[None], (comp_count,) + own.shape))
    d = lax.all_to_all(copies, "comp", 0, 0, tiled=True)
    ratio = jnp.stack([ratios, jnp.log2(ratios)], axis=0)

    own_pairs = lax.dynamic_slice_in_dim(slot_pair, me * own_slots, own_slots)
    ib, jb = slot_tables(own_pairs)
    ref = reference_blocks(observed, ib == jb, side)
    res, sent = device_kernel(ib, jb, ratio, station_uvw, d, ref, group_count)
    residual = res.reshape(chans, own_slots, 2 * side * side)
    got = lax.all_to_all(sent, ("comp", "freq"), 0, 0, tiled=True)
    flux_grad = jnp.sum(got, axis=(0, 1))
    return residual, flux_grad


def solution(mesh):
    in_specs = (P(), P(None, "comp"), P("comp"), P("comp"), P("freq"), P(), P("freq", "comp", None))
    out_specs = (P("freq", "comp", None), P("comp"))
    return jax.shard_map(body, mesh=mesh, in_specs=in_specs, out_specs=out_specs, check_vma=False)
```
